32 devices in a mesh: section: 8 (over z, y), tensor: 4 (over x, core).
Axes of the slice: x: 2, y: 2, z: 4, core: 2. Of those that a mesh axis runs over, the one named last changes fastest.
Arguments:
- inputs: bfloat16 [4, 16, 8192], P(None, 'section', 'tensor'), may hold values from -6 to 6
- cotangent: bfloat16 [4, 16, 8192], P(None, 'section', 'tensor'), may hold values from -1.5 to 1.5
- plan: int32 [4], replicated, may hold values from 0 to 3, each once
- weights: bfloat16 [8, 6656, 8192], P('section', None, 'tensor'), may hold values from -0.0625 to 0.0625
Outputs:
- grads: bfloat16 [8, 6656, 8192], P('section', None, 'tensor')
The draws below stay inside these ranges and needn't reach their ends.
Inputs may be any that keep to these rules, and one draw needn't show every extreme that they name: `plan`: a permutation of the 4 micro-batches.
All inputs are finite; a program needn't handle non-finite values.
Results may differ from the reference program's by a relative error of at most 0.028.
Values may be sent and summed in bfloat16 or wider, within the bound.
A program may use at most 384 MiB of HBM per device.

```python
import jax
import jax.numpy as jnp
from jax import lax

D = 8192
FS = 26624
MB = 4
ROWS = 16
COPIES = 4
PIECES = 8
FP = 6656
N_TENSOR = 4


def shard_levels(stream_key, extent, pieces, least, top_value):
    gain = 1.0
    for dim, parts in pieces:
        steps = jax.random.uniform(jax.random.fold_in(jax.random.fold_in(stream_key, 6), dim), (parts,), jnp.float32, least / len(pieces), top_value / len(pieces))
        gain = gain * jnp.repeat(jnp.exp(steps), extent[dim] // parts).reshape((-1,) + (1,) * (len(extent) - 1 - dim))
    return gain


def gaussian(stream_key, shape, width, limit, shards=(), kind=jnp.bfloat16):
    result = width * jax.random.normal(stream_key, shape, jnp.float32)
    if shards:
        result = result * shard_levels(stream_key, shape, shards, -0.22, 0.18)
    return jnp.clip(result, -limit, limit).astype(kind)


def setup_inputs(seed: int = 0) -> dict:
    key_list = jax.random.split(jax.random.key(seed), 5)
    return {
        "inputs": gaussian(key_list[0], (MB, ROWS, D), 1.0, 6.0, ((1, 8), (2, 4))),
        "cotangent": gaussian(key_list[1], (MB, ROWS, D), 0.1, 1.5, ((1, 8), (2, 4))),
        "plan": jax.random.permutation(key_list[2], MB).astype(jnp.int32),
        "weights": gaussian(key_list[3], (PIECES, FP, D), D ** -0.5, 0.0625, ((0, 8), (2, 4))),
    }


def grouped(values, weight):
    row_count = values.shape[0]
    group_width = D // N_TENSOR
    split_values = values.reshape(row_count, N_TENSOR, group_width).transpose(1, 0, 2)
    split_weight = weight.reshape(FS, N_TENSOR, group_width).transpose(1, 0, 2)

    def add_group(running, operands):
        partial_value = jnp.dot(operands[0], operands[1].T, preferred_element_type=jnp.float32)
        rounded = lax.optimization_barrier(partial_value.astype(jnp.bfloat16))
        return running + rounded.astype(jnp.float32), None

    running, unused = lax.scan(add_group, jnp.zeros((row_count, FS), jnp.float32), (split_values, split_weight))
    return running


def reference(inputs, cotangent, plan, weights):
    entering = jnp.take(inputs, plan, axis=0).reshape(MB * ROWS, D)
    returning = cotangent.reshape(MB * ROWS, D)
    gate_rows = weights[:COPIES].reshape(FS, D)
    down_rows = weights[COPIES:].reshape(FS, D)
    pre_sum = grouped(entering, gate_rows)
    hidden = jax.nn.silu(pre_sum).astype(jnp.bfloat16)
    grad_hidden = grouped(returning, down_rows).astype(jnp.bfloat16)
    logistic = jax.nn.sigmoid(pre_sum)
    slope = logistic * (1.0 + pre_sum * (1.0 - logistic))
    grad_pre = (grad_hidden.astype(jnp.float32) * slope).astype(jnp.bfloat16)
    grad_gate = jnp.dot(grad_pre.T, entering, preferred_element_type=jnp.float32).astype(jnp.bfloat16)
    grad_down = jnp.dot(hidden.T, returning, preferred_element_type=jnp.float32).astype(jnp.bfloat16)
    return jnp.concatenate([grad_gate, grad_down], axis=0).reshape(PIECES, FP, D)
```

```python
import functools

import jax
import jax.numpy as jnp
from jax import lax
from jax.experimental import pallas as pl
from jax.experimental.pallas import tpu as pltpu
from jax.sharding import PartitionSpec as P

MESH = pl.DeviceIdType.MESH
CHUNKS = 4


def unit_of(hidden):
    return hidden // 13 if hidden % (13 * 128) == 0 else 128


def chunk_bounds(hidden):
    unit = unit_of(hidden)
    units = hidden // unit
    count = min(CHUNKS, units)
    edges = [-(-units * c // count) for c in range(count + 1)]
    return [(low * unit, (high - low) * unit) for low, high in zip(edges, edges[1:])]


def exchange_kernel(
    sections, tensors, bounds, unit,
    mine_ref, weight_hbm, left_ref, right_ref,
    weight, gathered, part, partial_in, kept, swap_out, swap_in,
    weight_sem, gather_send, gather_recv, reduce_send, reduce_recv,
    swap_send, swap_recv, spread_send, spread_recv,
):
    position = lax.axis_index("section")
    rank = lax.axis_index("tensor")
    half = sections // 2
    lower = position < half
    mirror = lax.rem(position + half, sections)
    row_count = right_ref.shape[0]
    block_rows = row_count // tensors

    loads = []
    for c, (low, size) in enumerate(bounds):
        rows = pl.ds(low, size)
        load = pltpu.make_async_copy(weight_hbm.at[rows], weight.at[rows], weight_sem.at[c])
        load.start()
        loads.append(load)

    barrier = pltpu.get_barrier_semaphore()
    for step in range(1, sections):
        other = lax.rem(position + step, sections)
        pl.semaphore_signal(barrier, inc=1, device_id=(other, rank), device_id_type=MESH)
    for step in range(1, tensors):
        other = lax.rem(rank + step, tensors)
        pl.semaphore_signal(barrier, inc=1, device_id=(position, other), device_id_type=MESH)
    pl.semaphore_wait(barrier, sections + tensors - 2)

    gathers = []
    for step in range(1, sections):
        other = lax.rem(position + step, sections)
        copy = pltpu.make_async_remote_copy(
            src_ref=mine_ref.at[other // half],
            dst_ref=gathered.at[position],
            send_sem=gather_send.at[step],
            recv_sem=gather_recv.at[step],
            device_id=(other, rank),
            device_id_type=MESH,
        )
        copy.start()
        gathers.append(copy)
    gathered[position] = mine_ref[position // half]
    for copy in gathers:
        copy.wait_recv()
    shard_rows = gathered.shape[1] // 2
    for pair in range(sections // 2):
        stacked = []
        for source in (2 * pair, 2 * pair + 1):
            block = gathered[source].astype(jnp.float32)
            stacked.append(jnp.concatenate([block[:shard_rows], block[shard_rows:]], axis=1))
        rows = pl.ds(2 * pair * shard_rows, 2 * shard_rows)
        right_ref[rows, :] = jnp.concatenate(stacked, axis=0).astype(jnp.bfloat16)

    def project(c):
        low, size = bounds[c]
        loads[c].wait()

        def tile(index, carry):
            start = pl.multiple_of(low + index * unit, 128)
            product = lax.dot_general(
                right_ref[...], weight[pl.ds(start, unit), :],
                (((1,), (1,)), ((), ())), preferred_element_type=jnp.float32,
            ).astype(jnp.bfloat16)
            for t in range(tensors):
                part[t, :, pl.ds(start, unit)] = product[t * block_rows:(t + 1) * block_rows]
            return carry

        lax.fori_loop(0, size // unit, tile, 0)
        lanes = pl.ds(low, size)
        copies = []
        for step in range(1, tensors):
            other = lax.rem(rank + step, tensors)
            copy = pltpu.make_async_remote_copy(
                src_ref=part.at[other, :, lanes],
                dst_ref=partial_in.at[step, :, lanes],
                send_sem=reduce_send.at[c, step],
                recv_sem=reduce_recv.at[c, step],
                device_id=(position, other),
                device_id_type=MESH,
            )
            copy.start()
            copies.append(copy)
        return copies

    def reduce(c, copies):
        low, size = bounds[c]
        lanes = pl.ds(low, size)
        for copy in copies:
            copy.wait_recv()
        pre_sum = part[rank, :, lanes].astype(jnp.float32)
        for step in range(1, tensors):
            pre_sum = pre_sum + partial_in[step, :, lanes].astype(jnp.float32)
        kept[:, lanes] = pre_sum
        hidden = pre_sum * jax.nn.sigmoid(pre_sum)
        swap_out[:, lanes] = jnp.where(lower, hidden, pre_sum).astype(jnp.bfloat16)
        copy = pltpu.make_async_remote_copy(
            src_ref=swap_out.at[:, lanes],
            dst_ref=swap_in.at[:, lanes],
            send_sem=swap_send.at[c],
            recv_sem=swap_recv.at[c],
            device_id=(mirror, rank),
            device_id_type=MESH,
        )
        copy.start()
        return copy

    def finish(c, swap):
        low, size = bounds[c]
        lanes = pl.ds(low, size)
        swap.wait_recv()
        pre_sum = kept[:, lanes]
        logistic = jax.nn.sigmoid(pre_sum)
        slope = logistic * (1.0 + pre_sum * (1.0 - logistic))
        received = swap_in[:, lanes].astype(jnp.float32)
        left_ref[rank, :, lanes] = jnp.where(lower, received * slope, received).astype(jnp.bfloat16)
        copies = []
        for step in range(1, tensors):
            other = lax.rem(rank + step, tensors)
            copy = pltpu.make_async_remote_copy(
                src_ref=left_ref.at[rank, :, lanes],
                dst_ref=left_ref.at[rank, :, lanes],
                send_sem=spread_send.at[c, step],
                recv_sem=spread_recv.at[c, step],
                device_id=(position, other),
                device_id_type=MESH,
            )
            copy.start()
            copies.append(copy)
        return copies

    count = len(bounds)
    reductions, swaps, spreads = [], [], []
    for moment in range(count + 2):
        if moment < count:
            reductions.append(project(moment))
        if 0 <= moment - 1 < count:
            swaps.append(reduce(moment - 1, reductions[moment - 1]))
        if 0 <= moment - 2 < count:
            spreads.append(finish(moment - 2, swaps[moment - 2]))
    for copies in spreads:
        for copy in copies:
            copy.wait_recv()
    for copy in gathers + sum(reductions, []) + swaps + sum(spreads, []):
        copy.wait_send()


def gradient_kernel(left_ref, right_ref, out_ref):
    rows = right_ref.shape[0]
    left = left_ref[...].reshape(rows, left_ref.shape[2])
    out_ref[...] = lax.dot_general(
        left, right_ref[...], (((0,), (0,)), ((), ())), preferred_element_type=jnp.float32
    ).astype(out_ref.dtype)


def local(sections, tensors, inputs, cotangent, plan, weights):
    batches, tokens, columns = inputs.shape
    hidden = weights.shape[1]
    shard_rows = batches * tokens
    row_count = shard_rows * sections
    block_rows = row_count // tensors
    unit = unit_of(hidden)
    bounds = chunk_bounds(hidden)
    count = len(bounds)

    entering = []
    for k in range(batches):
        row = inputs[0]
        for micro in range(1, batches):
            row = jnp.where(plan[k] == micro, inputs[micro], row)
        entering.append(row)
    mine = jnp.stack([jnp.stack(entering), cotangent])
    mine = mine.reshape(2, shard_rows, 2, columns // 2).transpose(0, 2, 1, 3)
    mine = mine.reshape(2, 2 * shard_rows, columns // 2)

    dma = pltpu.SemaphoreType.DMA
    left, right = pl.pallas_call(
        functools.partial(exchange_kernel, sections, tensors, bounds, unit),
        out_shape=(
            jax.ShapeDtypeStruct((tensors, block_rows, hidden), jnp.bfloat16),
            jax.ShapeDtypeStruct((row_count, columns), jnp.bfloat16),
        ),
        in_specs=[pl.BlockSpec(memory_space=pltpu.VMEM), pl.BlockSpec(memory_space=pl.ANY)],
        out_specs=(pl.BlockSpec(memory_space=pltpu.VMEM), pl.BlockSpec(memory_space=pltpu.VMEM)),
        scratch_shapes=[
            pltpu.VMEM((hidden, columns), jnp.bfloat16),
            pltpu.VMEM((sections, 2 * shard_rows, columns // 2), jnp.bfloat16),
            pltpu.VMEM((tensors, block_rows, hidden), jnp.bfloat16),
            pltpu.VMEM((tensors, block_rows, hidden), jnp.bfloat16),
            pltpu.VMEM((block_rows, hidden), jnp.float32),
            pltpu.VMEM((block_rows, hidden), jnp.bfloat16),
            pltpu.VMEM((block_rows, hidden), jnp.bfloat16),
            dma((count,)),
            dma((sections,)),
            dma((sections,)),
            dma((count, tensors)),
            dma((count, tensors)),
            dma((count,)),
            dma((count,)),
            dma((count, tensors)),
            dma((count, tensors)),
        ],
        compiler_params=pltpu.CompilerParams(
            collective_id=0, has_side_effects=True, vmem_limit_bytes=56 * 1024 * 1024
        ),
        cost_estimate=pl.CostEstimate(
            flops=2 * row_count * hidden * columns,
            bytes_accessed=2 * hidden * columns,
            transcendentals=2 * block_rows * hidden,
        ),
    )(mine, weights[0])

    grads = pl.pallas_call(
        gradient_kernel,
        grid=(hidden // unit,),
        out_shape=jax.ShapeDtypeStruct((hidden, columns), jnp.bfloat16),
        in_specs=[
            pl.BlockSpec((tensors, block_rows, unit), lambda i: (0, 0, i)),
            pl.BlockSpec((row_count, columns), lambda i: (0, 0)),
        ],
        out_specs=pl.BlockSpec((unit, columns), lambda i: (i, 0)),
        compiler_params=pltpu.CompilerParams(vmem_limit_bytes=40 * 1024 * 1024),
        cost_estimate=pl.CostEstimate(
            flops=2 * row_count * hidden * columns,
            bytes_accessed=2 * hidden * columns,
            transcendentals=0,
        ),
    )(left, right)
    return grads.reshape(1, hidden, columns)


def solution(mesh):
    placed = (
        P(None, "section", "tensor"),
        P(None, "section", "tensor"),
        P(),
        P("section", None, "tensor"),
    )
    return jax.shard_map(
        functools.partial(local, mesh.shape["section"], mesh.shape["tensor"]),
        mesh=mesh, in_specs=placed, out_specs=P("section", None, "tensor"), check_vma=False,
    )
```

```python
import functools

import jax
import jax.numpy as jnp
from jax import lax
from jax.experimental import pallas as pl
from jax.experimental.pallas import tpu as pltpu
from jax.sharding import PartitionSpec as P

MESH = pl.DeviceIdType.MESH
CHUNKS = 5


def unit_of(hidden):
    return hidden // 13 if hidden % (13 * 128) == 0 else 128


def chunk_bounds(hidden):
    unit = unit_of(hidden)
    units = hidden // unit
    count = min(CHUNKS, units)
    edges = [-(-units * c // count) for c in range(count + 1)]
    return [(low * unit, (high - low) * unit) for low, high in zip(edges, edges[1:])]


def exchange_kernel(
    sections, tensors, bounds, unit,
    plan_ref, inputs_ref, cotangent_ref, weight_hbm, left_ref, right_ref,
    weight, stage, mine, gathered, part, pair_in, pair_sum, far_in, kept, swap_out, swap_in,
    weight_sem, gather_send, gather_recv, near_send, near_recv, far_send, far_recv,
    swap_send, swap_recv, wide_send, wide_recv, close_send, close_recv,
):
    position = lax.axis_index("section")
    rank = lax.axis_index("tensor")
    half = sections // 2
    lower = position < half
    mirror = lax.rem(position + half, sections)
    groups = tensors // 2
    parity = lax.rem(rank, 2)
    group = rank // 2
    buddy = rank + 1 - 2 * parity
    row_count = right_ref.shape[0]
    block_rows = row_count // tensors
    batches, tokens, columns = inputs_ref.shape

    barrier = pltpu.get_barrier_semaphore()
    for step in range(1, sections):
        other = lax.rem(position + step, sections)
        pl.semaphore_signal(barrier, inc=1, device_id=(other, rank), device_id_type=MESH)
    for step in range(1, groups):
        other = 2 * lax.rem(group + step, groups) + parity
        pl.semaphore_signal(barrier, inc=1, device_id=(position, other), device_id_type=MESH)
    pl.semaphore_signal(barrier, inc=1, device_id=(position, buddy), device_id_type=MESH)

    loads = []
    for c, (low, size) in enumerate(bounds):
        rows = pl.ds(low, size)
        load = pltpu.make_async_copy(weight_hbm.at[rows], weight.at[rows], weight_sem.at[c])
        load.start()
        loads.append(load)

    for k in range(batches):
        rows = pl.ds(k * tokens, tokens)
        stage[0, rows, :] = inputs_ref[plan_ref[k]].astype(jnp.float32)
        stage[1, rows, :] = cotangent_ref[k].astype(jnp.float32)
    for side in range(2):
        block = stage[side]
        mine[side] = jnp.concatenate(
            [block[:, :columns // 2], block[:, columns // 2:]], axis=0
        ).astype(jnp.bfloat16)

    pl.semaphore_wait(barrier, sections - 1 + groups)

    gathers = []
    for step in range(1, sections):
        other = lax.rem(position + step, sections)
        copy = pltpu.make_async_remote_copy(
            src_ref=mine.at[other // half],
            dst_ref=gathered.at[position],
            send_sem=gather_send.at[step],
            recv_sem=gather_recv.at[step],
            device_id=(other, rank),
            device_id_type=MESH,
        )
        copy.start()
        gathers.append(copy)
    gathered[position] = mine[position // half]
    for copy in gathers:
        copy.wait_recv()
    shard_rows = batches * tokens
    for pair in range(sections // 2):
        stacked = []
        for source in (2 * pair, 2 * pair + 1):
            block = gathered[source].astype(jnp.float32)
            stacked.append(jnp.concatenate([block[:shard_rows], block[shard_rows:]], axis=1))
        rows = pl.ds(2 * pair * shard_rows, 2 * shard_rows)
        right_ref[rows, :] = jnp.concatenate(stacked, axis=0).astype(jnp.bfloat16)

    def project(c):
        low, size = bounds[c]
        loads[c].wait()

        def tile(index, carry):
            start = pl.multiple_of(low + index * unit, 128)
            product = lax.dot_general(
                right_ref[...], weight[pl.ds(start, unit), :],
                (((1,), (1,)), ((), ())), preferred_element_type=jnp.float32,
            ).astype(jnp.bfloat16)
            for t in range(tensors):
                part[t % 2, t // 2, :, pl.ds(start, unit)] = product[t * block_rows:(t + 1) * block_rows]
            return carry

        lax.fori_loop(0, size // unit, tile, 0)
        lanes = pl.ds(low, size)
        copy = pltpu.make_async_remote_copy(
            src_ref=part.at[1 - parity, :, :, lanes],
            dst_ref=pair_in.at[:, :, lanes],
            send_sem=near_send.at[c],
            recv_sem=near_recv.at[c],
            device_id=(position, buddy),
            device_id_type=MESH,
        )
        copy.start()
        return copy

    def pair_up(c, near):
        low, size = bounds[c]
        lanes = pl.ds(low, size)
        near.wait_recv()
        copies = []
        for step in range(1, groups):
            other = lax.rem(group + step, groups)
            pair_sum[step, :, lanes] = (
                part[parity, other, :, lanes].astype(jnp.float32)
                + pair_in[other, :, lanes].astype(jnp.float32)
            ).astype(jnp.bfloat16)
            copy = pltpu.make_async_remote_copy(
                src_ref=pair_sum.at[step, :, lanes],
                dst_ref=far_in.at[step, :, lanes],
                send_sem=far_send.at[c, step],
                recv_sem=far_recv.at[c, step],
                device_id=(position, 2 * other + parity),
                device_id_type=MESH,
            )
            copy.start()
            copies.append(copy)
        return copies

    def reduce(c, far):
        low, size = bounds[c]
        lanes = pl.ds(low, size)
        pre_sum = part[parity, group, :, lanes].astype(jnp.float32)
        pre_sum = pre_sum + pair_in[group, :, lanes].astype(jnp.float32)
        for copy in far:
            copy.wait_recv()
        for step in range(1, groups):
            pre_sum = pre_sum + far_in[step, :, lanes].astype(jnp.float32)
        logistic = jax.nn.sigmoid(pre_sum)
        kept[:, lanes] = logistic * (1.0 + pre_sum * (1.0 - logistic))
        swap_out[:, lanes] = jnp.where(lower, pre_sum * logistic, pre_sum).astype(jnp.bfloat16)
        copy = pltpu.make_async_remote_copy(
            src_ref=swap_out.at[:, lanes],
            dst_ref=swap_in.at[:, lanes],
            send_sem=swap_send.at[c],
            recv_sem=swap_recv.at[c],
            device_id=(mirror, rank),
            device_id_type=MESH,
        )
        copy.start()
        return copy

    def hand_over(c, step):
        low, size = bounds[c]
        source = 2 * lax.rem(group - step + groups, groups) + parity
        block = left_ref.at[source, :, pl.ds(low, size)]
        copy = pltpu.make_async_remote_copy(
            src_ref=block,
            dst_ref=block,
            send_sem=close_send.at[c, step],
            recv_sem=close_recv.at[c, step],
            device_id=(position, buddy),
            device_id_type=MESH,
        )
        copy.start()
        return copy

    def finish(c, swap):
        low, size = bounds[c]
        lanes = pl.ds(low, size)
        swap.wait_recv()
        received = swap_in[:, lanes].astype(jnp.float32)
        left_ref[rank, :, lanes] = jnp.where(
            lower, received * kept[:, lanes], received
        ).astype(jnp.bfloat16)
        copies = []
        for step in range(1, groups):
            other = 2 * lax.rem(group + step, groups) + parity
            copy = pltpu.make_async_remote_copy(
                src_ref=left_ref.at[rank, :, lanes],
                dst_ref=left_ref.at[rank, :, lanes],
                send_sem=wide_send.at[c, step],
                recv_sem=wide_recv.at[c, step],
                device_id=(position, other),
                device_id_type=MESH,
            )
            copy.start()
            copies.append(copy)
        return copies, hand_over(c, 0)

    def forward(c, wide):
        copies = []
        for step in range(1, groups):
            wide[step - 1].wait_recv()
            copies.append(hand_over(c, step))
        return copies

    count = len(bounds)
    nears, fars, swaps, wides, closes = [], [], [], [], []
    for moment in range(count + 4):
        if moment < count:
            nears.append(project(moment))
        if 0 <= moment - 1 < count:
            fars.append(pair_up(moment - 1, nears[moment - 1]))
        if 0 <= moment - 2 < count:
            swaps.append(reduce(moment - 2, fars[moment - 2]))
        if 0 <= moment - 3 < count:
            wide, close = finish(moment - 3, swaps[moment - 3])
            wides.append(wide)
            closes.append(close)
        if 0 <= moment - 4 < count:
            closes.extend(forward(moment - 4, wides[moment - 4]))
    for copy in closes:
        copy.wait_recv()
    for copy in gathers + nears + sum(fars, []) + swaps + sum(wides, []) + closes:
        copy.wait_send()


SLOTS = 4


def gradient_kernel(height, left_ref, right_ref, out_hbm, tiles, sems):
    rows, columns = right_ref.shape
    count = out_hbm.shape[0] // height
    width = min(256, columns)

    def copy_out(index, slot):
        start = pl.multiple_of(index * height, height)
        return pltpu.make_async_copy(tiles.at[slot], out_hbm.at[pl.ds(start, height)], sems.at[slot])

    def tile(index, carry):
        slot = lax.rem(index, SLOTS)

        @pl.when(index >= SLOTS)
        def _():
            copy_out(index - SLOTS, slot).wait()

        start = pl.multiple_of(index * height, height)
        left = left_ref[:, :, pl.ds(start, height)].reshape(rows, height)
        for low in range(0, columns, width):
            tiles[slot, :, low:low + width] = lax.dot_general(
                left, right_ref[:, low:low + width],
                (((0,), (0,)), ((), ())), preferred_element_type=jnp.float32,
            ).astype(tiles.dtype)
        copy_out(index, slot).start()
        return carry

    lax.fori_loop(0, count, tile, 0)
    for index in range(max(0, count - SLOTS), count):
        copy_out(index, index % SLOTS).wait()


def local(sections, tensors, inputs, cotangent, plan, weights):
    batches, tokens, columns = inputs.shape
    hidden = weights.shape[1]
    shard_rows = batches * tokens
    row_count = shard_rows * sections
    block_rows = row_count // tensors
    groups = tensors // 2
    unit = unit_of(hidden)
    bounds = chunk_bounds(hidden)
    count = len(bounds)
    vmem = pl.BlockSpec(memory_space=pltpu.VMEM)

    dma = pltpu.SemaphoreType.DMA
    left, right = pl.pallas_call(
        functools.partial(exchange_kernel, sections, tensors, bounds, unit),
        out_shape=(
            jax.ShapeDtypeStruct((tensors, block_rows, hidden), jnp.bfloat16),
            jax.ShapeDtypeStruct((row_count, columns), jnp.bfloat16),
        ),
        in_specs=[pl.BlockSpec(memory_space=pltpu.SMEM), vmem, vmem, pl.BlockSpec(memory_space=pl.ANY)],
        out_specs=(vmem, vmem),
        scratch_shapes=[
            pltpu.VMEM((hidden, columns), jnp.bfloat16),
            pltpu.VMEM((2, shard_rows, columns), jnp.float32),
            pltpu.VMEM((2, 2 * shard_rows, columns // 2), jnp.bfloat16),
            pltpu.VMEM((sections, 2 * shard_rows, columns // 2), jnp.bfloat16),
            pltpu.VMEM((2, groups, block_rows, hidden), jnp.bfloat16),
            pltpu.VMEM((groups, block_rows, hidden), jnp.bfloat16),
            pltpu.VMEM((groups, block_rows, hidden), jnp.bfloat16),
            pltpu.VMEM((groups, block_rows, hidden), jnp.bfloat16),
            pltpu.VMEM((block_rows, hidden), jnp.float32),
            pltpu.VMEM((block_rows, hidden), jnp.bfloat16),
            pltpu.VMEM((block_rows, hidden), jnp.bfloat16),
            dma((count,)),
            dma((sections,)),
            dma((sections,)),
            dma((count,)),
            dma((count,)),
            dma((count, groups)),
            dma((count, groups)),
            dma((count,)),
            dma((count,)),
            dma((count, groups)),
            dma((count, groups)),
            dma((count, groups)),
            dma((count, groups)),
        ],
        compiler_params=pltpu.CompilerParams(
            collective_id=0, has_side_effects=True, vmem_limit_bytes=56 * 1024 * 1024
        ),
        cost_estimate=pl.CostEstimate(
            flops=2 * row_count * hidden * columns,
            bytes_accessed=2 * hidden * columns,
            transcendentals=2 * block_rows * hidden,
        ),
    )(plan, inputs, cotangent, weights[0])

    height = next(h for h in (256, 128) if hidden % h == 0)
    grads = pl.pallas_call(
        functools.partial(gradient_kernel, height),
        out_shape=jax.ShapeDtypeStruct((hidden, columns), jnp.bfloat16),
        in_specs=[vmem, vmem],
        out_specs=pl.BlockSpec(memory_space=pl.ANY),
        scratch_shapes=[pltpu.VMEM((SLOTS, height, columns), jnp.bfloat16), dma((SLOTS,))],
        compiler_params=pltpu.CompilerParams(vmem_limit_bytes=60 * 1024 * 1024),
        cost_estimate=pl.CostEstimate(
            flops=2 * row_count * hidden * columns,
            bytes_accessed=2 * hidden * columns,
            transcendentals=0,
        ),
    )(left, right)
    return grads.reshape(1, hidden, columns)


def solution(mesh):
    placed = (
        P(None, "section", "tensor"),
        P(None, "section", "tensor"),
        P(),
        P("section", None, "tensor"),
    )
    return jax.shard_map(
        functools.partial(local, mesh.shape["section"], mesh.shape["tensor"]),
        mesh=mesh, in_specs=placed, out_specs=P("section", None, "tensor"), check_vma=False,
    )
```

```python
import functools

import jax
import jax.numpy as jnp
from jax import lax
from jax.experimental import pallas as pl
from jax.experimental.pallas import tpu as pltpu
from jax.sharding import PartitionSpec as P

MESH = pl.DeviceIdType.MESH
CHUNKS = 5


def unit_of(hidden):
    return hidden // 13 if hidden % (13 * 128) == 0 else 128


def chunk_bounds(hidden):
    unit = unit_of(hidden)
    units = hidden // unit
    count = min(CHUNKS, units)
    edges = [-(-units * c // count) for c in range(count + 1)]
    return [(low * unit, (high - low) * unit) for low, high in zip(edges, edges[1:])]


def exchange_kernel(
    sections, tensors, bounds, unit,
    plan_ref, inputs_ref, cotangent_ref, weight_hbm, left_ref, right_ref,
    weight, stage, mine, gathered, part, pair_in, pair_sum, far_in, kept, swap_out, swap_in,
    weight_sem, gather_send, gather_recv, near_send, near_recv, far_send, far_recv,
    swap_send, swap_recv, wide_send, wide_recv, close_send, close_recv,
):
    position = lax.axis_index("section")
    rank = lax.axis_index("tensor")
    half = sections // 2
    lower = position < half
    mirror = lax.rem(position + half, sections)
    groups = tensors // 2
    parity = lax.rem(rank, 2)
    group = rank // 2
    buddy = rank + 1 - 2 * parity
    row_count = right_ref.shape[0]
    block_rows = row_count // tensors
    batches, tokens, columns = inputs_ref.shape

    barrier = pltpu.get_barrier_semaphore()
    for step in range(1, sections):
        other = lax.rem(position + step, sections)
        pl.semaphore_signal(barrier, inc=1, device_id=(other, rank), device_id_type=MESH)
    for step in range(1, groups):
        other = 2 * lax.rem(group + step, groups) + parity
        pl.semaphore_signal(barrier, inc=1, device_id=(position, other), device_id_type=MESH)
    pl.semaphore_signal(barrier, inc=1, device_id=(position, buddy), device_id_type=MESH)

    loads = []
    for c, (low, size) in enumerate(bounds):
        rows = pl.ds(low, size)
        load = pltpu.make_async_copy(weight_hbm.at[rows], weight.at[rows], weight_sem.at[c])
        load.start()
        loads.append(load)

    for k in range(batches):
        rows = pl.ds(k * tokens, tokens)
        stage[0, rows, :] = inputs_ref[plan_ref[k]].astype(jnp.float32)
        stage[1, rows, :] = cotangent_ref[k].astype(jnp.float32)
    for side in range(2):
        block = stage[side]
        mine[side] = jnp.concatenate(
            [block[:, :columns // 2], block[:, columns // 2:]], axis=0
        ).astype(jnp.bfloat16)

    pl.semaphore_wait(barrier, sections - 1 + groups)

    gathers = []
    for step in range(1, sections):
        other = lax.rem(position + step, sections)
        copy = pltpu.make_async_remote_copy(
            src_ref=mine.at[other // half],
            dst_ref=gathered.at[position],
            send_sem=gather_send.at[step],
            recv_sem=gather_recv.at[step],
            device_id=(other, rank),
            device_id_type=MESH,
        )
        copy.start()
        gathers.append(copy)
    gathered[position] = mine[position // half]
    for copy in gathers:
        copy.wait_recv()
    shard_rows = batches * tokens
    for pair in range(sections // 2):
        stacked = []
        for source in (2 * pair, 2 * pair + 1):
            block = gathered[source].astype(jnp.float32)
            stacked.append(jnp.concatenate([block[:shard_rows], block[shard_rows:]], axis=1))
        rows = pl.ds(2 * pair * shard_rows, 2 * shard_rows)
        right_ref[rows, :] = jnp.concatenate(stacked, axis=0).astype(jnp.bfloat16)

    def project(c):
        low, size = bounds[c]
        loads[c].wait()

        def tile(index, carry):
            start = pl.multiple_of(low + index * unit, 128)
            product = lax.dot_general(
                weight[pl.ds(start, unit), :], right_ref[...],
                (((1,), (1,)), ((), ())), preferred_element_type=jnp.float32,
            ).T.astype(jnp.bfloat16)
            for t in range(tensors):
                part[t % 2, t // 2, :, pl.ds(start, unit)] = product[t * block_rows:(t + 1) * block_rows]
            return carry

        lax.fori_loop(0, size // unit, tile, 0)
        lanes = pl.ds(low, size)
        copy = pltpu.make_async_remote_copy(
            src_ref=part.at[1 - parity, :, :, lanes],
            dst_ref=pair_in.at[:, :, lanes],
            send_sem=near_send.at[c],
            recv_sem=near_recv.at[c],
            device_id=(position, buddy),
            device_id_type=MESH,
        )
        copy.start()
        return copy

    def pair_up(c, near):
        low, size = bounds[c]
        lanes = pl.ds(low, size)
        near.wait_recv()
        copies = []
        for step in range(1, groups):
            other = lax.rem(group + step, groups)
            pair_sum[step, :, lanes] = (
                part[parity, other, :, lanes].astype(jnp.float32)
                + pair_in[other, :, lanes].astype(jnp.float32)
            ).astype(jnp.bfloat16)
            copy = pltpu.make_async_remote_copy(
                src_ref=pair_sum.at[step, :, lanes],
                dst_ref=far_in.at[step, :, lanes],
                send_sem=far_send.at[c, step],
                recv_sem=far_recv.at[c, step],
                device_id=(position, 2 * other + parity),
                device_id_type=MESH,
            )
            copy.start()
            copies.append(copy)
        return copies

    def reduce(c, far):
        low, size = bounds[c]
        lanes = pl.ds(low, size)
        pre_sum = part[parity, group, :, lanes].astype(jnp.float32)
        pre_sum = pre_sum + pair_in[group, :, lanes].astype(jnp.float32)
        for copy in far:
            copy.wait_recv()
        for step in range(1, groups):
            pre_sum = pre_sum + far_in[step, :, lanes].astype(jnp.float32)
        logistic = jax.nn.sigmoid(pre_sum)
        kept[:, lanes] = logistic * (1.0 + pre_sum * (1.0 - logistic))
        swap_out[:, lanes] = jnp.where(lower, pre_sum * logistic, pre_sum).astype(jnp.bfloat16)
        copy = pltpu.make_async_remote_copy(
            src_ref=swap_out.at[:, lanes],
            dst_ref=swap_in.at[:, lanes],
            send_sem=swap_send.at[c],
            recv_sem=swap_recv.at[c],
            device_id=(mirror, rank),
            device_id_type=MESH,
        )
        copy.start()
        return copy

    def hand_over(c, step):
        low, size = bounds[c]
        source = 2 * lax.rem(group - step + groups, groups) + parity
        block = left_ref.at[source, :, pl.ds(low, size)]
        copy = pltpu.make_async_remote_copy(
            src_ref=block,
            dst_ref=block,
            send_sem=close_send.at[c, step],
            recv_sem=close_recv.at[c, step],
            device_id=(position, buddy),
            device_id_type=MESH,
        )
        copy.start()
        return copy

    def finish(c, swap):
        low, size = bounds[c]
        lanes = pl.ds(low, size)
        swap.wait_recv()
        received = swap_in[:, lanes].astype(jnp.float32)
        left_ref[rank, :, lanes] = jnp.where(
            lower, received * kept[:, lanes], received
        ).astype(jnp.bfloat16)
        copies = []
        for step in range(1, groups):
            other = 2 * lax.rem(group + step, groups) + parity
            copy = pltpu.make_async_remote_copy(
                src_ref=left_ref.at[rank, :, lanes],
                dst_ref=left_ref.at[rank, :, lanes],
                send_sem=wide_send.at[c, step],
                recv_sem=wide_recv.at[c, step],
                device_id=(position, other),
                device_id_type=MESH,
            )
            copy.start()
            copies.append(copy)
        return copies, hand_over(c, 0)

    def forward(c, wide):
        copies = []
        for step in range(1, groups):
            wide[step - 1].wait_recv()
            copies.append(hand_over(c, step))
        return copies

    count = len(bounds)
    nears, fars, swaps, wides, closes = [], [], [], [], []
    for moment in range(count + 4):
        if moment < count:
            nears.append(project(moment))
        if 0 <= moment - 1 < count:
            fars.append(pair_up(moment - 1, nears[moment - 1]))
        if 0 <= moment - 2 < count:
            swaps.append(reduce(moment - 2, fars[moment - 2]))
        if 0 <= moment - 3 < count:
            wide, close = finish(moment - 3, swaps[moment - 3])
            wides.append(wide)
            closes.append(close)
        if 0 <= moment - 4 < count:
            closes.extend(forward(moment - 4, wides[moment - 4]))
    for copy in closes:
        copy.wait_recv()
    for copy in gathers + nears + sum(fars, []) + swaps + sum(wides, []) + closes:
        copy.wait_send()


def local(sections, tensors, inputs, cotangent, plan, weights):
    batches, tokens, columns = inputs.shape
    hidden = weights.shape[1]
    shard_rows = batches * tokens
    row_count = shard_rows * sections
    block_rows = row_count // tensors
    groups = tensors // 2
    unit = unit_of(hidden)
    bounds = chunk_bounds(hidden)
    count = len(bounds)
    vmem = pl.BlockSpec(memory_space=pltpu.VMEM)

    dma = pltpu.SemaphoreType.DMA
    left, right = pl.pallas_call(
        functools.partial(exchange_kernel, sections, tensors, bounds, unit),
        out_shape=(
            jax.ShapeDtypeStruct((tensors, block_rows, hidden), jnp.bfloat16),
            jax.ShapeDtypeStruct((row_count, columns), jnp.bfloat16),
        ),
        in_specs=[pl.BlockSpec(memory_space=pltpu.SMEM), vmem, vmem, pl.BlockSpec(memory_space=pl.ANY)],
        out_specs=(vmem, vmem),
        scratch_shapes=[
            pltpu.VMEM((hidden, columns), jnp.bfloat16),
            pltpu.VMEM((2, shard_rows, columns), jnp.float32),
            pltpu.VMEM((2, 2 * shard_rows, columns // 2), jnp.bfloat16),
            pltpu.VMEM((sections, 2 * shard_rows, columns // 2), jnp.bfloat16),
            pltpu.VMEM((2, groups, block_rows, hidden), jnp.bfloat16),
            pltpu.VMEM((groups, block_rows, hidden), jnp.bfloat16),
            pltpu.VMEM((groups, block_rows, hidden), jnp.bfloat16),
            pltpu.VMEM((groups, block_rows, hidden), jnp.bfloat16),
            pltpu.VMEM((block_rows, hidden), jnp.float32),
            pltpu.VMEM((block_rows, hidden), jnp.bfloat16),
            pltpu.VMEM((block_rows, hidden), jnp.bfloat16),
            dma((count,)),
            dma((sections,)),
            dma((sections,)),
            dma((count,)),
            dma((count,)),
            dma((count, groups)),
            dma((count, groups)),
            dma((count,)),
            dma((count,)),
            dma((count, groups)),
            dma((count, groups)),
            dma((count, groups)),
            dma((count, groups)),
        ],
        compiler_params=pltpu.CompilerParams(
            collective_id=0, has_side_effects=True, vmem_limit_bytes=56 * 1024 * 1024
        ),
        cost_estimate=pl.CostEstimate(
            flops=2 * row_count * hidden * columns,
            bytes_accessed=2 * hidden * columns,
            transcendentals=2 * block_rows * hidden,
        ),
    )(plan, inputs, cotangent, weights[0])

    grads = lax.dot_general(
        left.reshape(row_count, hidden), right, (((0,), (0,)), ((), ())),
        preferred_element_type=jnp.float32,
    ).astype(jnp.bfloat16)
    return grads.reshape(1, hidden, columns)


def solution(mesh):
    placed = (
        P(None, "section", "tensor"),
        P(None, "section", "tensor"),
        P(),
        P("section", None, "tensor"),
    )
    return jax.shard_map(
        functools.partial(local, mesh.shape["section"], mesh.shape["tensor"]),
        mesh=mesh, in_specs=placed, out_specs=P("section", None, "tensor"), check_vma=False,
    )
```

```python
import functools

import jax
import jax.numpy as jnp
from jax import lax
from jax.experimental import pallas as pl
from jax.experimental.pallas import tpu as pltpu
from jax.sharding import PartitionSpec as P

MESH = pl.DeviceIdType.MESH
CHUNKS = 7
EARLY = 3


def unit_of(hidden):
    return hidden // 13 if hidden % (13 * 128) == 0 else 128


def chunk_bounds(hidden):
    unit = unit_of(hidden)
    units = hidden // unit
    count = min(CHUNKS, units)
    edges = [-(-units * c // count) for c in range(count + 1)]
    return [(low * unit, (high - low) * unit) for low, high in zip(edges, edges[1:])]


def exchange_kernel(
    sections, tensors, bounds, unit,
    plan_ref, inputs_ref, cotangent_ref, weight_hbm, left_ref, right_ref, early_hbm,
    weight, stage, mine, gathered, part, pair_in, pair_sum, far_in, kept, swap_out, swap_in, tiles,
    weight_sem, gather_send, gather_recv, near_send, near_recv, far_send, far_recv,
    swap_send, swap_recv, wide_send, wide_recv, close_send, close_recv, early_sem,
):
    position = lax.axis_index("section")
    rank = lax.axis_index("tensor")
    half = sections // 2
    lower = position < half
    mirror = lax.rem(position + half, sections)
    groups = tensors // 2
    parity = lax.rem(rank, 2)
    group = rank // 2
    buddy = rank + 1 - 2 * parity
    row_count = right_ref.shape[0]
    block_rows = row_count // tensors
    batches, tokens, columns = inputs_ref.shape

    barrier = pltpu.get_barrier_semaphore()
    for step in range(1, sections):
        other = lax.rem(position + step, sections)
        pl.semaphore_signal(barrier, inc=1, device_id=(other, rank), device_id_type=MESH)
    for step in range(1, groups):
        other = 2 * lax.rem(group + step, groups) + parity
        pl.semaphore_signal(barrier, inc=1, device_id=(position, other), device_id_type=MESH)
    pl.semaphore_signal(barrier, inc=1, device_id=(position, buddy), device_id_type=MESH)

    def load(index):
        rows = pl.ds(pl.multiple_of(index * unit, 128), unit)
        return pltpu.make_async_copy(weight_hbm.at[rows], weight.at[rows], weight_sem.at[index])

    for index in range(weight.shape[0] // unit):
        load(index).start()

    for k in range(batches):
        rows = pl.ds(k * tokens, tokens)
        stage[0, rows, :] = inputs_ref[plan_ref[k]].astype(jnp.float32)
        stage[1, rows, :] = cotangent_ref[k].astype(jnp.float32)
    for side in range(2):
        block = stage[side]
        mine[side] = jnp.concatenate(
            [block[:, :columns // 2], block[:, columns // 2:]], axis=0
        ).astype(jnp.bfloat16)

    pl.semaphore_wait(barrier, sections - 1 + groups)

    gathers = []
    for step in range(1, sections):
        other = lax.rem(position + step, sections)
        copy = pltpu.make_async_remote_copy(
            src_ref=mine.at[other // half],
            dst_ref=gathered.at[position],
            send_sem=gather_send.at[step],
            recv_sem=gather_recv.at[step],
            device_id=(other, rank),
            device_id_type=MESH,
        )
        copy.start()
        gathers.append(copy)
    gathered[position] = mine[position // half]
    for copy in gathers:
        copy.wait_recv()
    shard_rows = batches * tokens
    for pair in range(sections // 2):
        stacked = []
        for source in (2 * pair, 2 * pair + 1):
            block = gathered[source].astype(jnp.float32)
            stacked.append(jnp.concatenate([block[:shard_rows], block[shard_rows:]], axis=1))
        rows = pl.ds(2 * pair * shard_rows, 2 * shard_rows)
        right_ref[rows, :] = jnp.concatenate(stacked, axis=0).astype(jnp.bfloat16)

    def project(c):
        low, size = bounds[c]

        def tile(index, carry):
            load(low // unit + index).wait()
            start = pl.multiple_of(low + index * unit, 128)
            product = lax.dot_general(
                weight[pl.ds(start, unit), :], right_ref[...],
                (((1,), (1,)), ((), ())), preferred_element_type=jnp.float32,
            ).T.astype(jnp.bfloat16)
            for t in range(tensors):
                part[t % 2, t // 2, :, pl.ds(start, unit)] = product[t * block_rows:(t + 1) * block_rows]
            return carry

        lax.fori_loop(0, size // unit, tile, 0)
        lanes = pl.ds(low, size)
        copy = pltpu.make_async_remote_copy(
            src_ref=part.at[1 - parity, :, :, lanes],
            dst_ref=pair_in.at[:, :, lanes],
            send_sem=near_send.at[c],
            recv_sem=near_recv.at[c],
            device_id=(position, buddy),
            device_id_type=MESH,
        )
        copy.start()
        return copy

    def pair_up(c, near):
        low, size = bounds[c]
        lanes = pl.ds(low, size)
        near.wait_recv()
        copies = []
        for step in range(1, groups):
            other = lax.rem(group + step, groups)
            pair_sum[step, :, lanes] = (
                part[parity, other, :, lanes].astype(jnp.float32)
                + pair_in[other, :, lanes].astype(jnp.float32)
            ).astype(jnp.bfloat16)
            copy = pltpu.make_async_remote_copy(
                src_ref=pair_sum.at[step, :, lanes],
                dst_ref=far_in.at[step, :, lanes],
                send_sem=far_send.at[c, step],
                recv_sem=far_recv.at[c, step],
                device_id=(position, 2 * other + parity),
                device_id_type=MESH,
            )
            copy.start()
            copies.append(copy)
        return copies

    def reduce(c, far):
        low, size = bounds[c]
        lanes = pl.ds(low, size)
        pre_sum = part[parity, group, :, lanes].astype(jnp.float32)
        pre_sum = pre_sum + pair_in[group, :, lanes].astype(jnp.float32)
        for copy in far:
            copy.wait_recv()
        for step in range(1, groups):
            pre_sum = pre_sum + far_in[step, :, lanes].astype(jnp.float32)
        logistic = jax.nn.sigmoid(pre_sum)
        kept[:, lanes] = logistic * (1.0 + pre_sum * (1.0 - logistic))
        swap_out[:, lanes] = jnp.where(lower, pre_sum * logistic, pre_sum).astype(jnp.bfloat16)
        copy = pltpu.make_async_remote_copy(
            src_ref=swap_out.at[:, lanes],
            dst_ref=swap_in.at[:, lanes],
            send_sem=swap_send.at[c],
            recv_sem=swap_recv.at[c],
            device_id=(mirror, rank),
            device_id_type=MESH,
        )
        copy.start()
        return copy

    def hand_over(c, step):
        low, size = bounds[c]
        source = 2 * lax.rem(group - step + groups, groups) + parity
        block = left_ref.at[source, :, pl.ds(low, size)]
        copy = pltpu.make_async_remote_copy(
            src_ref=block,
            dst_ref=block,
            send_sem=close_send.at[c, step],
            recv_sem=close_recv.at[c, step],
            device_id=(position, buddy),
            device_id_type=MESH,
        )
        copy.start()
        return copy

    def finish(c, swap):
        low, size = bounds[c]
        lanes = pl.ds(low, size)
        swap.wait_recv()
        received = swap_in[:, lanes].astype(jnp.float32)
        left_ref[rank, :, lanes] = jnp.where(
            lower, received * kept[:, lanes], received
        ).astype(jnp.bfloat16)
        copies = []
        for step in range(1, groups):
            other = 2 * lax.rem(group + step, groups) + parity
            copy = pltpu.make_async_remote_copy(
                src_ref=left_ref.at[rank, :, lanes],
                dst_ref=left_ref.at[rank, :, lanes],
                send_sem=wide_send.at[c, step],
                recv_sem=wide_recv.at[c, step],
                device_id=(position, other),
                device_id_type=MESH,
            )
            copy.start()
            copies.append(copy)
        return copies, hand_over(c, 0)

    def forward(c, wide):
        copies = []
        for step in range(1, groups):
            wide[step - 1].wait_recv()
            copies.append(hand_over(c, step))
        return copies

    def early_tile(index):
        def store(low, width, value):
            tiles[index, :, low:low + width] = value

        outer_tile(left_ref, right_ref, index * unit, unit, store)
        copy = pltpu.make_async_copy(
            tiles.at[index], early_hbm.at[pl.ds(index * unit, unit)], early_sem.at[index]
        )
        copy.start()
        return copy

    count = len(bounds)
    arrived = 0
    nears, fars, swaps, wides, closes, earlies = [], [], [], [], [], []
    for moment in range(count + 4):
        if moment < count:
            nears.append(project(moment))
        if 0 <= moment - 1 < count:
            fars.append(pair_up(moment - 1, nears[moment - 1]))
        if 0 <= moment - 2 < count:
            swaps.append(reduce(moment - 2, fars[moment - 2]))
        if 0 <= moment - 3 < count:
            wide, close = finish(moment - 3, swaps[moment - 3])
            wides.append(wide)
            closes.append([close])
        if 0 <= moment - 4 < count:
            closes[moment - 4].extend(forward(moment - 4, wides[moment - 4]))
        if moment >= count and len(earlies) < EARLY:
            while sum(size for _, size in bounds[:arrived]) < (len(earlies) + 1) * unit:
                for copy in closes[arrived]:
                    copy.wait_recv()
                arrived += 1
            earlies.append(early_tile(len(earlies)))
    for copy in sum(closes[arrived:], []):
        copy.wait_recv()
    sent = gathers + nears + sum(fars, []) + swaps + sum(wides, []) + sum(closes, [])
    for copy in sent:
        copy.wait_send()
    for copy in earlies:
        copy.wait()


def outer_tile(left_ref, right_ref, start, height, store):
    rows, columns = right_ref.shape
    width = min(256, columns)
    left = left_ref[:, :, pl.ds(start, height)].reshape(rows, height)
    for low in range(0, columns, width):
        store(low, width, lax.dot_general(
            left, right_ref[:, low:low + width],
            (((0,), (0,)), ((), ())), preferred_element_type=jnp.float32,
        ).astype(jnp.bfloat16))


SLOTS = 4


def gradient_kernel(height, left_ref, right_ref, early_hbm, out_hbm, tiles, held, sems, held_in, held_out):
    ready = held.shape[0]
    count = (out_hbm.shape[0] - ready) // height

    def copy_out(index, slot):
        start = pl.multiple_of(ready + index * height, 128)
        return pltpu.make_async_copy(tiles.at[slot], out_hbm.at[pl.ds(start, height)], sems.at[slot])

    def tile(index, carry):
        slot = lax.rem(index, SLOTS)

        @pl.when(index >= SLOTS)
        def _():
            copy_out(index - SLOTS, slot).wait()

        def store(low, width, value):
            tiles[slot, :, low:low + width] = value

        start = pl.multiple_of(ready + index * height, 128)
        outer_tile(left_ref, right_ref, start, height, store)
        copy_out(index, slot).start()
        return carry

    bring = pltpu.make_async_copy(early_hbm, held, held_in)
    bring.start()
    split = count // 2
    lax.fori_loop(0, split, tile, 0)
    bring.wait()
    put = pltpu.make_async_copy(held, out_hbm.at[pl.ds(0, ready)], held_out)
    put.start()
    lax.fori_loop(split, count, tile, 0)
    for index in range(max(0, count - SLOTS), count):
        copy_out(index, index % SLOTS).wait()
    put.wait()


def local(sections, tensors, inputs, cotangent, plan, weights):
    batches, tokens, columns = inputs.shape
    hidden = weights.shape[1]
    shard_rows = batches * tokens
    row_count = shard_rows * sections
    block_rows = row_count // tensors
    groups = tensors // 2
    unit = unit_of(hidden)
    bounds = chunk_bounds(hidden)
    count = len(bounds)
    ready = EARLY * unit
    vmem = pl.BlockSpec(memory_space=pltpu.VMEM)

    dma = pltpu.SemaphoreType.DMA
    left, right, early = pl.pallas_call(
        functools.partial(exchange_kernel, sections, tensors, bounds, unit),
        out_shape=(
            jax.ShapeDtypeStruct((tensors, block_rows, hidden), jnp.bfloat16),
            jax.ShapeDtypeStruct((row_count, columns), jnp.bfloat16),
            jax.ShapeDtypeStruct((ready, columns), jnp.bfloat16),
        ),
        in_specs=[pl.BlockSpec(memory_space=pltpu.SMEM), vmem, vmem, pl.BlockSpec(memory_space=pl.ANY)],
        out_specs=(vmem, vmem, pl.BlockSpec(memory_space=pl.ANY)),
        scratch_shapes=[
            pltpu.VMEM((hidden, columns), jnp.bfloat16),
            pltpu.VMEM((2, shard_rows, columns), jnp.float32),
            pltpu.VMEM((2, 2 * shard_rows, columns // 2), jnp.bfloat16),
            pltpu.VMEM((sections, 2 * shard_rows, columns // 2), jnp.bfloat16),
            pltpu.VMEM((2, groups, block_rows, hidden), jnp.bfloat16),
            pltpu.VMEM((groups, block_rows, hidden), jnp.bfloat16),
            pltpu.VMEM((groups, block_rows, hidden), jnp.bfloat16),
            pltpu.VMEM((groups, block_rows, hidden), jnp.bfloat16),
            pltpu.VMEM((block_rows, hidden), jnp.float32),
            pltpu.VMEM((block_rows, hidden), jnp.bfloat16),
            pltpu.VMEM((block_rows, hidden), jnp.bfloat16),
            pltpu.VMEM((EARLY, unit, columns), jnp.bfloat16),
            dma((hidden // unit,)),
            dma((sections,)),
            dma((sections,)),
            dma((count,)),
            dma((count,)),
            dma((count, groups)),
            dma((count, groups)),
            dma((count,)),
            dma((count,)),
            dma((count, groups)),
            dma((count, groups)),
            dma((count, groups)),
            dma((count, groups)),
            dma((EARLY,)),
        ],
        compiler_params=pltpu.CompilerParams(
            collective_id=0, has_side_effects=True, vmem_limit_bytes=56 * 1024 * 1024
        ),
        cost_estimate=pl.CostEstimate(
            flops=2 * row_count * hidden * columns,
            bytes_accessed=2 * hidden * columns,
            transcendentals=2 * block_rows * hidden,
        ),
    )(plan, inputs, cotangent, weights[0])

    height = next(h for h in (256, 128) if (hidden - ready) % h == 0)
    grads = pl.pallas_call(
        functools.partial(gradient_kernel, height),
        out_shape=jax.ShapeDtypeStruct((hidden, columns), jnp.bfloat16),
        in_specs=[vmem, vmem, pl.BlockSpec(memory_space=pl.ANY)],
        out_specs=pl.BlockSpec(memory_space=pl.ANY),
        scratch_shapes=[
            pltpu.VMEM((SLOTS, height, columns), jnp.bfloat16),
            pltpu.VMEM((ready, columns), jnp.bfloat16),
            dma((SLOTS,)),
            dma,
            dma,
        ],
        compiler_params=pltpu.CompilerParams(vmem_limit_bytes=60 * 1024 * 1024),
        cost_estimate=pl.CostEstimate(
            flops=2 * row_count * hidden * columns,
            bytes_accessed=2 * hidden * columns,
            transcendentals=0,
        ),
    )(left, right, early)
    return grads.reshape(1, hidden, columns)


def solution(mesh):
    placed = (
        P(None, "section", "tensor"),
        P(None, "section", "tensor"),
        P(),
        P("section", None, "tensor"),
    )
    return jax.shard_map(
        functools.partial(local, mesh.shape["section"], mesh.shape["tensor"]),
        mesh=mesh, in_specs=placed, out_specs=P("section", None, "tensor"), check_vma=False,
    )
```

```python
import functools

import jax
import jax.numpy as jnp
from jax import lax
from jax.experimental import pallas as pl
from jax.experimental.pallas import tpu as pltpu
from jax.sharding import PartitionSpec as P

MESH = pl.DeviceIdType.MESH
SLOTS = 3


def unit_of(hidden):
    return hidden // 13 if hidden % (13 * 128) == 0 else 128


def chunk_bounds(hidden):
    size = 1664 if hidden % 1664 == 0 else unit_of(hidden)
    return [(low, size) for low in range(0, hidden, size)]


def exchange_kernel(
    sections, tensors, bounds, unit,
    plan_ref, inputs_ref, cotangent_ref, weight_hbm, left_ref, right_ref,
    weight, stage, mine, gathered, part, pair_in, pair_sum, far_in, kept, swap_out, swap_in,
    weight_sem, gather_send, gather_recv, near_send, near_recv, far_send, far_recv,
    swap_send, swap_recv, wide_send, wide_recv, close_send, close_recv,
):
    position = lax.axis_index("section")
    rank = lax.axis_index("tensor")
    half = sections // 2
    lower = position < half
    mirror = lax.rem(position + half, sections)
    groups = tensors // 2
    parity = lax.rem(rank, 2)
    group = rank // 2
    buddy = rank + 1 - 2 * parity
    row_count = right_ref.shape[0]
    block_rows = row_count // tensors
    batches, tokens, columns = inputs_ref.shape

    barrier = pltpu.get_barrier_semaphore()
    for step in range(1, sections):
        other = lax.rem(position + step, sections)
        pl.semaphore_signal(barrier, inc=1, device_id=(other, rank), device_id_type=MESH)
    for step in range(1, groups):
        other = 2 * lax.rem(group + step, groups) + parity
        pl.semaphore_signal(barrier, inc=1, device_id=(position, other), device_id_type=MESH)
    pl.semaphore_signal(barrier, inc=1, device_id=(position, buddy), device_id_type=MESH)

    loads = []
    for c, (low, size) in enumerate(bounds):
        rows = pl.ds(low, size)
        load = pltpu.make_async_copy(weight_hbm.at[rows], weight.at[rows], weight_sem.at[c])
        load.start()
        loads.append(load)

    for k in range(batches):
        rows = pl.ds(k * tokens, tokens)
        stage[0, rows, :] = inputs_ref[plan_ref[k]].astype(jnp.float32)
        stage[1, rows, :] = cotangent_ref[k].astype(jnp.float32)
    for side in range(2):
        block = stage[side]
        mine[side] = jnp.concatenate(
            [block[:, :columns // 2], block[:, columns // 2:]], axis=0
        ).astype(jnp.bfloat16)

    pl.semaphore_wait(barrier, sections - 1 + groups)

    gathers = []
    for step in range(1, sections):
        other = lax.rem(position + step, sections)
        copy = pltpu.make_async_remote_copy(
            src_ref=mine.at[other // half],
            dst_ref=gathered.at[position],
            send_sem=gather_send.at[step],
            recv_sem=gather_recv.at[step],
            device_id=(other, rank),
            device_id_type=MESH,
        )
        copy.start()
        gathers.append(copy)
    gathered[position] = mine[position // half]
    for copy in gathers:
        copy.wait_recv()
    shard_rows = batches * tokens
    for pair in range(sections // 2):
        stacked = []
        for source in (2 * pair, 2 * pair + 1):
            block = gathered[source].astype(jnp.float32)
            stacked.append(jnp.concatenate([block[:shard_rows], block[shard_rows:]], axis=1))
        rows = pl.ds(2 * pair * shard_rows, 2 * shard_rows)
        right_ref[rows, :] = jnp.concatenate(stacked, axis=0).astype(jnp.bfloat16)

    def project(c):
        low, size = bounds[c]
        loads[c].wait()

        product = lax.dot_general(
            weight[pl.ds(low, size), :], right_ref[...],
            (((1,), (1,)), ((), ())), preferred_element_type=jnp.float32,
        ).T.astype(jnp.bfloat16)
        for t in range(tensors):
            part[t % 2, t // 2, :, pl.ds(low, size)] = product[t * block_rows:(t + 1) * block_rows]
        lanes = pl.ds(low, size)
        copy = pltpu.make_async_remote_copy(
            src_ref=part.at[1 - parity, :, :, lanes],
            dst_ref=pair_in.at[:, :, lanes],
            send_sem=near_send.at[c],
            recv_sem=near_recv.at[c],
            device_id=(position, buddy),
            device_id_type=MESH,
        )
        copy.start()
        return copy

    def pair_up(c, near):
        low, size = bounds[c]
        lanes = pl.ds(low, size)
        near.wait_recv()
        copies = []
        for step in range(1, groups):
            other = lax.rem(group + step, groups)
            pair_sum[step, :, lanes] = (
                part[parity, other, :, lanes].astype(jnp.float32)
                + pair_in[other, :, lanes].astype(jnp.float32)
            ).astype(jnp.bfloat16)
            copy = pltpu.make_async_remote_copy(
                src_ref=pair_sum.at[step, :, lanes],
                dst_ref=far_in.at[step, :, lanes],
                send_sem=far_send.at[c, step],
                recv_sem=far_recv.at[c, step],
                device_id=(position, 2 * other + parity),
                device_id_type=MESH,
            )
            copy.start()
            copies.append(copy)
        return copies

    def reduce(c, far):
        low, size = bounds[c]
        lanes = pl.ds(low, size)
        pre_sum = part[parity, group, :, lanes].astype(jnp.float32)
        pre_sum = pre_sum + pair_in[group, :, lanes].astype(jnp.float32)
        for copy in far:
            copy.wait_recv()
        for step in range(1, groups):
            pre_sum = pre_sum + far_in[step, :, lanes].astype(jnp.float32)
        logistic = jax.nn.sigmoid(pre_sum)
        kept[:, lanes] = logistic * (1.0 + pre_sum * (1.0 - logistic))
        swap_out[:, lanes] = jnp.where(lower, pre_sum * logistic, pre_sum).astype(jnp.bfloat16)
        copy = pltpu.make_async_remote_copy(
            src_ref=swap_out.at[:, lanes],
            dst_ref=swap_in.at[:, lanes],
            send_sem=swap_send.at[c],
            recv_sem=swap_recv.at[c],
            device_id=(mirror, rank),
            device_id_type=MESH,
        )
        copy.start()
        return copy

    def hand_over(c, step):
        low, size = bounds[c]
        source = 2 * lax.rem(group - step + groups, groups) + parity
        block = left_ref.at[source, :, pl.ds(low, size)]
        copy = pltpu.make_async_remote_copy(
            src_ref=block,
            dst_ref=block,
            send_sem=close_send.at[c, step],
            recv_sem=close_recv.at[c, step],
            device_id=(position, buddy),
            device_id_type=MESH,
        )
        copy.start()
        return copy

    def finish(c, swap):
        low, size = bounds[c]
        lanes = pl.ds(low, size)
        swap.wait_recv()
        received = swap_in[:, lanes].astype(jnp.float32)
        left_ref[rank, :, lanes] = jnp.where(
            lower, received * kept[:, lanes], received
        ).astype(jnp.bfloat16)
        copies = []
        for step in range(1, groups):
            other = 2 * lax.rem(group + step, groups) + parity
            copy = pltpu.make_async_remote_copy(
                src_ref=left_ref.at[rank, :, lanes],
                dst_ref=left_ref.at[rank, :, lanes],
                send_sem=wide_send.at[c, step],
                recv_sem=wide_recv.at[c, step],
                device_id=(position, other),
                device_id_type=MESH,
            )
            copy.start()
            copies.append(copy)
        return copies, hand_over(c, 0)

    def forward(c, wide):
        copies = []
        for step in range(1, groups):
            wide[step - 1].wait_recv()
            copies.append(hand_over(c, step))
        return copies

    count = len(bounds)
    nears, fars, swaps, wides, closes = [], [], [], [], []
    for moment in range(count + 4):
        if moment < count:
            nears.append(project(moment))
        if 0 <= moment - 1 < count:
            fars.append(pair_up(moment - 1, nears[moment - 1]))
        if 0 <= moment - 2 < count:
            swaps.append(reduce(moment - 2, fars[moment - 2]))
        if 0 <= moment - 3 < count:
            wide, close = finish(moment - 3, swaps[moment - 3])
            wides.append(wide)
            closes.append(close)
        if 0 <= moment - 4 < count:
            closes.extend(forward(moment - 4, wides[moment - 4]))
    for copy in closes:
        copy.wait_recv()
    for copy in gathers + nears + sum(fars, []) + swaps + sum(wides, []) + closes:
        copy.wait_send()


def gradient_kernel(height, left_ref, right_ref, out_hbm, tiles, sems):
    rows, columns = right_ref.shape
    hidden = out_hbm.shape[0]
    count = hidden // height
    rest = hidden - count * height
    width = min(256, columns)

    def copy_out(index, slot, size=height):
        start = pl.multiple_of(index * height, 128)
        return pltpu.make_async_copy(
            tiles.at[slot, pl.ds(0, size)], out_hbm.at[pl.ds(start, size)], sems.at[slot]
        )

    def fill(index, slot, size):
        start = pl.multiple_of(index * height, 128)
        left = left_ref[:, :, pl.ds(start, size)].reshape(rows, size)
        for low in range(0, columns, width):
            tiles[slot, pl.ds(0, size), low:low + width] = lax.dot_general(
                left, right_ref[:, low:low + width],
                (((0,), (0,)), ((), ())), preferred_element_type=jnp.float32,
            ).astype(tiles.dtype)

    def tile(index, carry):
        slot = lax.rem(index, SLOTS)

        @pl.when(index >= SLOTS)
        def _():
            copy_out(index - SLOTS, slot).wait()

        fill(index, slot, height)
        copy_out(index, slot).start()
        return carry

    lax.fori_loop(0, count, tile, 0)
    first = max(0, count - SLOTS)
    if rest:
        if count >= SLOTS:
            copy_out(first, first % SLOTS).wait()
            first += 1
        fill(count, count % SLOTS, rest)
        copy_out(count, count % SLOTS, rest).start()
    for index in range(first, count):
        copy_out(index, index % SLOTS).wait()
    if rest:
        copy_out(count, count % SLOTS, rest).wait()


def local(sections, tensors, inputs, cotangent, plan, weights):
    batches, tokens, columns = inputs.shape
    hidden = weights.shape[1]
    shard_rows = batches * tokens
    row_count = shard_rows * sections
    block_rows = row_count // tensors
    groups = tensors // 2
    unit = unit_of(hidden)
    bounds = chunk_bounds(hidden)
    count = len(bounds)
    vmem = pl.BlockSpec(memory_space=pltpu.VMEM)

    dma = pltpu.SemaphoreType.DMA
    left, right = pl.pallas_call(
        functools.partial(exchange_kernel, sections, tensors, bounds, unit),
        out_shape=(
            jax.ShapeDtypeStruct((tensors, block_rows, hidden), jnp.bfloat16),
            jax.ShapeDtypeStruct((row_count, columns), jnp.bfloat16),
        ),
        in_specs=[pl.BlockSpec(memory_space=pltpu.SMEM), vmem, vmem, pl.BlockSpec(memory_space=pl.ANY)],
        out_specs=(vmem, vmem),
        scratch_shapes=[
            pltpu.VMEM((hidden, columns), jnp.bfloat16),
            pltpu.VMEM((2, shard_rows, columns), jnp.float32),
            pltpu.VMEM((2, 2 * shard_rows, columns // 2), jnp.bfloat16),
            pltpu.VMEM((sections, 2 * shard_rows, columns // 2), jnp.bfloat16),
            pltpu.VMEM((2, groups, block_rows, hidden), jnp.bfloat16),
            pltpu.VMEM((groups, block_rows, hidden), jnp.bfloat16),
            pltpu.VMEM((groups, block_rows, hidden), jnp.bfloat16),
            pltpu.VMEM((groups, block_rows, hidden), jnp.bfloat16),
            pltpu.VMEM((block_rows, hidden), jnp.float32),
            pltpu.VMEM((block_rows, hidden), jnp.bfloat16),
            pltpu.VMEM((block_rows, hidden), jnp.bfloat16),
            dma((count,)),
            dma((sections,)),
            dma((sections,)),
            dma((count,)),
            dma((count,)),
            dma((count, groups)),
            dma((count, groups)),
            dma((count,)),
            dma((count,)),
            dma((count, groups)),
            dma((count, groups)),
            dma((count, groups)),
            dma((count, groups)),
        ],
        compiler_params=pltpu.CompilerParams(
            collective_id=0, has_side_effects=True, vmem_limit_bytes=56 * 1024 * 1024
        ),
        cost_estimate=pl.CostEstimate(
            flops=2 * row_count * hidden * columns,
            bytes_accessed=2 * hidden * columns,
            transcendentals=2 * block_rows * hidden,
        ),
    )(plan, inputs, cotangent, weights[0])

    height = 2 * unit
    grads = pl.pallas_call(
        functools.partial(gradient_kernel, height),
        out_shape=jax.ShapeDtypeStruct((hidden, columns), jnp.bfloat16),
        in_specs=[vmem, vmem],
        out_specs=pl.BlockSpec(memory_space=pl.ANY),
        scratch_shapes=[pltpu.VMEM((SLOTS, height, columns), jnp.bfloat16), dma((SLOTS,))],
        compiler_params=pltpu.CompilerParams(vmem_limit_bytes=60 * 1024 * 1024),
        cost_estimate=pl.CostEstimate(
            flops=2 * row_count * hidden * columns,
            bytes_accessed=2 * hidden * columns,
            transcendentals=0,
        ),
    )(left, right)
    return grads.reshape(1, hidden, columns)


def solution(mesh):
    placed = (
        P(None, "section", "tensor"),
        P(None, "section", "tensor"),
        P(),
        P("section", None, "tensor"),
    )
    return jax.shard_map(
        functools.partial(local, mesh.shape["section"], mesh.shape["tensor"]),
        mesh=mesh, in_specs=placed, out_specs=P("section", None, "tensor"), check_vma=False,
    )
```

```python
import functools

import jax
import jax.numpy as jnp
from jax import lax
from jax.experimental import pallas as pl
from jax.experimental.pallas import tpu as pltpu
from jax.sharding import PartitionSpec as P

MESH = pl.DeviceIdType.MESH
CHUNKS = 5
SLOTS = 3


def unit_of(hidden):
    return hidden // 13 if hidden % (13 * 128) == 0 else 128


def chunk_bounds(hidden):
    unit = unit_of(hidden)
    units = hidden // unit
    count = min(CHUNKS, units)
    edges = [-(-units * c // count) for c in range(count + 1)]
    return [(low * unit, (high - low) * unit) for low, high in zip(edges, edges[1:])]


def exchange_kernel(
    sections, tensors, bounds, unit,
    plan_ref, inputs_ref, cotangent_ref, weight_hbm, left_ref, right_ref,
    weight, stage, mine, gathered, part, pair_in, pair_sum, far_in, kept, swap_out, swap_in,
    weight_sem, gather_send, gather_recv, near_send, near_recv, far_send, far_recv,
    swap_send, swap_recv, wide_send, wide_recv, close_send, close_recv,
):
    position = lax.axis_index("section")
    rank = lax.axis_index("tensor")
    half = sections // 2
    lower = position < half
    mirror = lax.rem(position + half, sections)
    groups = tensors // 2
    parity = lax.rem(rank, 2)
    group = rank // 2
    buddy = rank + 1 - 2 * parity
    row_count = right_ref.shape[0]
    block_rows = row_count // tensors
    batches, tokens, columns = inputs_ref.shape

    barrier = pltpu.get_barrier_semaphore()
    for step in range(1, sections):
        other = lax.rem(position + step, sections)
        pl.semaphore_signal(barrier, inc=1, device_id=(other, rank), device_id_type=MESH)
    for step in range(1, groups):
        other = 2 * lax.rem(group + step, groups) + parity
        pl.semaphore_signal(barrier, inc=1, device_id=(position, other), device_id_type=MESH)
    pl.semaphore_signal(barrier, inc=1, device_id=(position, buddy), device_id_type=MESH)

    loads = []
    for c, (low, size) in enumerate(bounds):
        rows = pl.ds(low, size)
        load = pltpu.make_async_copy(weight_hbm.at[rows], weight.at[rows], weight_sem.at[c])
        load.start()
        loads.append(load)

    for k in range(batches):
        rows = pl.ds(k * tokens, tokens)
        stage[0, rows, :] = inputs_ref[plan_ref[k]].astype(jnp.float32)
        stage[1, rows, :] = cotangent_ref[k].astype(jnp.float32)
    for side in range(2):
        block = stage[side]
        mine[side] = jnp.concatenate(
            [block[:, :columns // 2], block[:, columns // 2:]], axis=0
        ).astype(jnp.bfloat16)

    pl.semaphore_wait(barrier, sections - 1 + groups)

    gathers = []
    for step in range(1, sections):
        other = lax.rem(position + step, sections)
        copy = pltpu.make_async_remote_copy(
            src_ref=mine.at[other // half],
            dst_ref=gathered.at[position],
            send_sem=gather_send.at[step],
            recv_sem=gather_recv.at[step],
            device_id=(other, rank),
            device_id_type=MESH,
        )
        copy.start()
        gathers.append(copy)
    gathered[position] = mine[position // half]
    for copy in gathers:
        copy.wait_recv()
    shard_rows = batches * tokens
    for pair in range(sections // 2):
        stacked = []
        for source in (2 * pair, 2 * pair + 1):
            block = gathered[source].astype(jnp.float32)
            stacked.append(jnp.concatenate([block[:shard_rows], block[shard_rows:]], axis=1))
        rows = pl.ds(2 * pair * shard_rows, 2 * shard_rows)
        right_ref[rows, :] = jnp.concatenate(stacked, axis=0).astype(jnp.bfloat16)

    def project(c):
        low, size = bounds[c]
        loads[c].wait()

        def tile(index, carry):
            start = pl.multiple_of(low + index * unit, 128)
            product = lax.dot_general(
                weight[pl.ds(start, unit), :], right_ref[...],
                (((1,), (1,)), ((), ())), preferred_element_type=jnp.float32,
            ).T.astype(jnp.bfloat16)
            for t in range(tensors):
                part[t % 2, t // 2, :, pl.ds(start, unit)] = product[t * block_rows:(t + 1) * block_rows]
            return carry

        lax.fori_loop(0, size // unit, tile, 0)
        lanes = pl.ds(low, size)
        copy = pltpu.make_async_remote_copy(
            src_ref=part.at[1 - parity, :, :, lanes],
            dst_ref=pair_in.at[:, :, lanes],
            send_sem=near_send.at[c],
            recv_sem=near_recv.at[c],
            device_id=(position, buddy),
            device_id_type=MESH,
        )
        copy.start()
        return copy

    def pair_up(c, near):
        low, size = bounds[c]
        lanes = pl.ds(low, size)
        near.wait_recv()
        copies = []
        for step in range(1, groups):
            other = lax.rem(group + step, groups)
            pair_sum[step, :, lanes] = (
                part[parity, other, :, lanes].astype(jnp.float32)
                + pair_in[other, :, lanes].astype(jnp.float32)
            ).astype(jnp.bfloat16)
            copy = pltpu.make_async_remote_copy(
                src_ref=pair_sum.at[step, :, lanes],
                dst_ref=far_in.at[step, :, lanes],
                send_sem=far_send.at[c, step],
                recv_sem=far_recv.at[c, step],
                device_id=(position, 2 * other + parity),
                device_id_type=MESH,
            )
            copy.start()
            copies.append(copy)
        return copies

    def reduce(c, far):
        low, size = bounds[c]
        lanes = pl.ds(low, size)
        pre_sum = part[parity, group, :, lanes].astype(jnp.float32)
        pre_sum = pre_sum + pair_in[group, :, lanes].astype(jnp.float32)
        for copy in far:
            copy.wait_recv()
        for step in range(1, groups):
            pre_sum = pre_sum + far_in[step, :, lanes].astype(jnp.float32)
        logistic = jax.nn.sigmoid(pre_sum)
        kept[:, lanes] = logistic * (1.0 + pre_sum * (1.0 - logistic))
        swap_out[:, lanes] = jnp.where(lower, pre_sum * logistic, pre_sum).astype(jnp.bfloat16)
        copy = pltpu.make_async_remote_copy(
            src_ref=swap_out.at[:, lanes],
            dst_ref=swap_in.at[:, lanes],
            send_sem=swap_send.at[c],
            recv_sem=swap_recv.at[c],
            device_id=(mirror, rank),
            device_id_type=MESH,
        )
        copy.start()
        return copy

    def hand_over(c, step):
        low, size = bounds[c]
        source = 2 * lax.rem(group - step + groups, groups) + parity
        block = left_ref.at[source, :, pl.ds(low, size)]
        copy = pltpu.make_async_remote_copy(
            src_ref=block,
            dst_ref=block,
            send_sem=close_send.at[c, step],
            recv_sem=close_recv.at[c, step],
            device_id=(position, buddy),
            device_id_type=MESH,
        )
        copy.start()
        return copy

    def finish(c, swap):
        low, size = bounds[c]
        lanes = pl.ds(low, size)
        swap.wait_recv()
        received = swap_in[:, lanes].astype(jnp.float32)
        left_ref[rank, :, lanes] = jnp.where(
            lower, received * kept[:, lanes], received
        ).astype(jnp.bfloat16)
        copies = []
        for step in range(1, groups):
            other = 2 * lax.rem(group + step, groups) + parity
            copy = pltpu.make_async_remote_copy(
                src_ref=left_ref.at[rank, :, lanes],
                dst_ref=left_ref.at[rank, :, lanes],
                send_sem=wide_send.at[c, step],
                recv_sem=wide_recv.at[c, step],
                device_id=(position, other),
                device_id_type=MESH,
            )
            copy.start()
            copies.append(copy)
        return copies, hand_over(c, 0)

    def forward(c, wide):
        copies = []
        for step in range(1, groups):
            wide[step - 1].wait_recv()
            copies.append(hand_over(c, step))
        return copies

    count = len(bounds)
    nears, fars, swaps, wides, closes = [], [], [], [], []
    for moment in range(count + 4):
        if moment < count:
            nears.append(project(moment))
        if 0 <= moment - 1 < count:
            fars.append(pair_up(moment - 1, nears[moment - 1]))
        if 0 <= moment - 2 < count:
            swaps.append(reduce(moment - 2, fars[moment - 2]))
        if 0 <= moment - 3 < count:
            wide, close = finish(moment - 3, swaps[moment - 3])
            wides.append(wide)
            closes.append(close)
        if 0 <= moment - 4 < count:
            closes.extend(forward(moment - 4, wides[moment - 4]))
    for copy in closes:
        copy.wait_recv()
    for copy in gathers + nears + sum(fars, []) + swaps + sum(wides, []) + closes:
        copy.wait_send()


def gradient_kernel(height, left_ref, right_ref, out_hbm, tiles, sems):
    rows, columns = right_ref.shape
    hidden = out_hbm.shape[0]
    count = hidden // height
    rest = hidden - count * height
    width = min(256, columns)

    def copy_out(index, slot, size=height):
        start = pl.multiple_of(index * height, 128)
        return pltpu.make_async_copy(
            tiles.at[slot, pl.ds(0, size)], out_hbm.at[pl.ds(start, size)], sems.at[slot]
        )

    def fill(index, slot, size):
        start = pl.multiple_of(index * height, 128)
        left = left_ref[:, :, pl.ds(start, size)].reshape(rows, size)
        for low in range(0, columns, width):
            tiles[slot, pl.ds(0, size), low:low + width] = lax.dot_general(
                left, right_ref[:, low:low + width],
                (((0,), (0,)), ((), ())), preferred_element_type=jnp.float32,
            ).astype(tiles.dtype)

    def tile(index, carry):
        slot = lax.rem(index, SLOTS)

        @pl.when(index >= SLOTS)
        def _():
            copy_out(index - SLOTS, slot).wait()

        fill(index, slot, height)
        copy_out(index, slot).start()
        return carry

    lax.fori_loop(0, count, tile, 0)
    first = max(0, count - SLOTS)
    if rest:
        if count >= SLOTS:
            copy_out(first, first % SLOTS).wait()
            first += 1
        fill(count, count % SLOTS, rest)
        copy_out(count, count % SLOTS, rest).start()
    for index in range(first, count):
        copy_out(index, index % SLOTS).wait()
    if rest:
        copy_out(count, count % SLOTS, rest).wait()


def local(sections, tensors, inputs, cotangent, plan, weights):
    batches, tokens, columns = inputs.shape
    hidden = weights.shape[1]
    shard_rows = batches * tokens
    row_count = shard_rows * sections
    block_rows = row_count // tensors
    groups = tensors // 2
    unit = unit_of(hidden)
    bounds = chunk_bounds(hidden)
    count = len(bounds)
    vmem = pl.BlockSpec(memory_space=pltpu.VMEM)

    dma = pltpu.SemaphoreType.DMA
    left, right = pl.pallas_call(
        functools.partial(exchange_kernel, sections, tensors, bounds, unit),
        out_shape=(
            jax.ShapeDtypeStruct((tensors, block_rows, hidden), jnp.bfloat16),
            jax.ShapeDtypeStruct((row_count, columns), jnp.bfloat16),
        ),
        in_specs=[pl.BlockSpec(memory_space=pltpu.SMEM), vmem, vmem, pl.BlockSpec(memory_space=pl.ANY)],
        out_specs=(vmem, vmem),
        scratch_shapes=[
            pltpu.VMEM((hidden, columns), jnp.bfloat16),
            pltpu.VMEM((2, shard_rows, columns), jnp.float32),
            pltpu.VMEM((2, 2 * shard_rows, columns // 2), jnp.bfloat16),
            pltpu.VMEM((sections, 2 * shard_rows, columns // 2), jnp.bfloat16),
            pltpu.VMEM((2, groups, block_rows, hidden), jnp.bfloat16),
            pltpu.VMEM((groups, block_rows, hidden), jnp.bfloat16),
            pltpu.VMEM((groups, block_rows, hidden), jnp.bfloat16),
            pltpu.VMEM((groups, block_rows, hidden), jnp.bfloat16),
            pltpu.VMEM((block_rows, hidden), jnp.float32),
            pltpu.VMEM((block_rows, hidden), jnp.bfloat16),
            pltpu.VMEM((block_rows, hidden), jnp.bfloat16),
            dma((count,)),
            dma((sections,)),
            dma((sections,)),
            dma((count,)),
            dma((count,)),
            dma((count, groups)),
            dma((count, groups)),
            dma((count,)),
            dma((count,)),
            dma((count, groups)),
            dma((count, groups)),
            dma((count, groups)),
            dma((count, groups)),
        ],
        compiler_params=pltpu.CompilerParams(
            collective_id=0, has_side_effects=True, vmem_limit_bytes=56 * 1024 * 1024
        ),
        cost_estimate=pl.CostEstimate(
            flops=2 * row_count * hidden * columns,
            bytes_accessed=2 * hidden * columns,
            transcendentals=2 * block_rows * hidden,
        ),
    )(plan, inputs, cotangent, weights[0])

    height = 2 * unit
    grads = pl.pallas_call(
        functools.partial(gradient_kernel, height),
        out_shape=jax.ShapeDtypeStruct((hidden, columns), jnp.bfloat16),
        in_specs=[vmem, vmem],
        out_specs=pl.BlockSpec(memory_space=pl.ANY),
        scratch_shapes=[pltpu.VMEM((SLOTS, height, columns), jnp.bfloat16), dma((SLOTS,))],
        compiler_params=pltpu.CompilerParams(vmem_limit_bytes=60 * 1024 * 1024),
        cost_estimate=pl.CostEstimate(
            flops=2 * row_count * hidden * columns,
            bytes_accessed=2 * hidden * columns,
            transcendentals=0,
        ),
    )(left, right)
    return grads.reshape(1, hidden, columns)


def solution(mesh):
    placed = (
        P(None, "section", "tensor"),
        P(None, "section", "tensor"),
        P(),
        P("section", None, "tensor"),
    )
    return jax.shard_map(
        functools.partial(local, mesh.shape["section"], mesh.shape["tensor"]),
        mesh=mesh, in_specs=placed, out_specs=P("section", None, "tensor"), check_vma=False,
    )
```
